32 devices in a mesh: act: 8 (over y, x, core), pix: 4 (over z).
Axes of the slice: x: 2, y: 2, z: 4, core: 2. Of those that a mesh axis runs over, the one named last changes fastest.
Arguments:
- pixel_index: int32 [4, 512], P('pix'), may hold values from 0 to 65535
- act_map: int32 [32768], P('act'), may hold values from 0 to 32767, each once
- omega: bfloat16 [32768, 128], P('act'), may hold values from -6 to 6
- pupil_field: float32 [4, 2, 32768], P('pix', None, 'act'), may hold values from -6 to 6
- channel_scale: float32 [4], P('pix'), may hold values from 0.9 to 1.1
- channel_flux: float32 [4], P('pix'), may hold values from 0.3 to 3
Outputs:
- basis_out: float32 [4, 1024, 128], P('pix', 'act')
- projection: float32 [128, 32768], P('pix', 'act')
- r_factor: float32 [128, 128], replicated
The draws below stay inside these ranges and needn't reach their ends.
Inputs may be any that keep to these rules, and one draw needn't show every extreme that they name: `act_map`: every number of 0 to 32767 appears once. `pixel_index`: pixels of a channel may repeat.
All inputs are finite; a program needn't handle non-finite values.
Results may differ from the reference program's by a relative error of at most 0.0048.
Values may be sent and summed in bfloat16 or wider, within the bound.
A program may use at most 64 MiB of HBM per device.

```python
import math
import jax
import jax.numpy as jnp
from jax import lax

GRID = 128
FOCAL = 256
RANK = 128
PIX = 512
ACT = 32768
CHANNELS = 4
ROWS = 4096


def place_ends(array, stream_key, smallest, top_value):
    spot = [jax.random.randint(jax.random.fold_in(stream_key, axis), (), 0, length) for axis, length in enumerate(array.shape)]
    main_axis = array.shape.index(max(array.shape))
    beside = spot[:main_axis] + [(spot[main_axis] + 1) % array.shape[main_axis]] + spot[main_axis + 1:]
    return array.at[tuple(spot)].set(smallest).at[tuple(beside)].set(top_value)


def steps_of(key, dims, split, low, high):
    factor_of = 1.0
    for position, blocks in split:
        steps = jax.random.uniform(jax.random.fold_in(jax.random.fold_in(key, 6), position), (blocks,), jnp.float32, low / len(split), high / len(split))
        factor_of = factor_of * jnp.repeat(jnp.exp(steps), dims[position] // blocks).reshape((-1,) + (1,) * (len(dims) - 1 - position))
    return factor_of


def noise(rng, extent, scale, most, split=(), kind=jnp.bfloat16):
    array = jax.random.normal(rng, extent, jnp.float32) * scale
    if len(split) > 0:
        array = steps_of(rng, extent, split, -0.22, 0.18) * array
    return jnp.clip(array, min=-most, max=most).astype(kind)


def setup_inputs(seed: int = 0) -> dict:
    key_list = jax.random.split(jax.random.key(seed), 7)
    pixel_index = place_ends(jax.random.randint(key_list[0], (CHANNELS, PIX), 0, FOCAL * FOCAL), jax.random.fold_in(key_list[0], 1), 0, (FOCAL * FOCAL) - 1).astype(jnp.int32)
    act_map = jax.random.permutation(key_list[1], ACT).astype(jnp.int32)
    omega = noise(key_list[2], (ACT, RANK), 1.0, 6.0, ((0, 8),))
    pupil_field = noise(key_list[3], (CHANNELS, 2, ACT), 1.0, 6.0, ((0, 4), (2, 8)), jnp.float32)
    channel_scale = jnp.clip(0.9 + 0.20000005 * jax.random.uniform(key_list[4], (CHANNELS,), jnp.float32) ** steps_of(key_list[4], (CHANNELS,), ((0, 4),), -0.2, 0.2), 0.9, 1.1)
    channel_flux = jnp.clip(jnp.exp(math.log(3.0) - 2.3025851 * jax.random.uniform(key_list[5], (CHANNELS,), jnp.float32) ** steps_of(key_list[5], (CHANNELS,), ((0, 4),), -0.2, 0.2)), 0.3, 3.0)
    return dict(pixel_index=pixel_index, act_map=act_map, omega=omega, pupil_field=pupil_field, channel_scale=channel_scale, channel_flux=channel_flux)


TWO_PI = 2.0 * math.pi
INFL_RATE = 4.5
DEFOCUS_RATE = 6.0

def jacobian_rows(pixels, wave_scale, flux_level, codes, field_re, field_im):
    delta_u = pixels // FOCAL - FOCAL // 2
    delta_v = pixels % FOCAL - FOCAL // 2
    mirror = codes // (GRID * GRID)
    column_x = codes // GRID % GRID - GRID // 2
    column_y = codes % GRID - GRID // 2
    phase_int = delta_u[:, None] * column_x[None, :] + delta_v[:, None] * column_y[None, :]
    radius = (delta_u * delta_u + delta_v * delta_v).astype(jnp.float32)
    amplitude = flux_level * jnp.exp(-INFL_RATE * radius / (FOCAL * FOCAL))
    defocus = radius * (TWO_PI * DEFOCUS_RATE / (FOCAL * FOCAL)) / wave_scale
    phase_angle = mirror.astype(jnp.float32)[None, :] * defocus[:, None] - TWO_PI / FOCAL * wave_scale * phase_int.astype(jnp.float32)
    cosine = jnp.cos(phase_angle)
    sine_part = jnp.sin(phase_angle)
    real_part = amplitude[:, None] * (field_re[None, :] * cosine - field_im[None, :] * sine_part)
    imag_part = amplitude[:, None] * (field_re[None, :] * sine_part + field_im[None, :] * cosine)
    stacked = jnp.stack([real_part, imag_part], axis=1)
    return stacked.reshape(2 * pixels.shape[0], codes.shape[0]).astype(jnp.bfloat16)

def reference(pixel_index, act_map, omega, pupil_field, channel_scale, channel_flux):
    block_cols = min(1024, ACT)
    block_count = ACT // block_cols
    codes_b = act_map.reshape(block_count, block_cols)
    omega_b = omega.reshape(block_count, block_cols, RANK)
    field_b = pupil_field.reshape(CHANNELS, 2, block_count, block_cols)

    def channel_block(chan_id, block_id):
        return jacobian_rows(pixel_index[chan_id], channel_scale[chan_id], channel_flux[chan_id], codes_b[block_id], field_b[chan_id, 0, block_id], field_b[chan_id, 1, block_id])

    def channel_sketch(chan_id):

        def add_block(accum_sum, block_id):
            jacobian = channel_block(chan_id, block_id)
            return (accum_sum + jnp.dot(jacobian.astype(jnp.float32), omega_b[block_id].astype(jnp.float32), preferred_element_type=jnp.float32), None)
        accum_sum, unused = lax.scan(add_block, jnp.zeros((2 * PIX, RANK), jnp.float32), jnp.arange(block_count, dtype=jnp.int32))
        return accum_sum
    sketch = lax.map(channel_sketch, jnp.arange(CHANNELS, dtype=jnp.int32)).reshape(ROWS, RANK)
    gram_matrix = lax.dot_general(sketch.astype(jnp.float32), sketch.astype(jnp.float32), (((0,), (0,)), ((), ())), precision=lax.Precision.HIGHEST, preferred_element_type=jnp.float32)
    lower_factor = jnp.linalg.cholesky(gram_matrix)
    basis = jax.scipy.linalg.solve_triangular(lower_factor, sketch.T, lower=True).T
    coarse = basis.astype(jnp.bfloat16).reshape(CHANNELS, 2 * PIX, RANK)

    def block_projection(block_id):

        def add_channel(accum_sum, chan_id):
            jacobian = channel_block(chan_id, block_id)
            term = lax.dot_general(coarse[chan_id].astype(jnp.float32), jacobian.astype(jnp.float32), (((0,), (0,)), ((), ())), preferred_element_type=jnp.float32)
            return (accum_sum + term, None)
        accum_sum, unused = lax.scan(add_channel, jnp.zeros((RANK, block_cols), jnp.float32), jnp.arange(CHANNELS, dtype=jnp.int32))
        return accum_sum
    blocks = lax.map(block_projection, jnp.arange(block_count, dtype=jnp.int32))
    projection = jnp.transpose(blocks, (1, 0, 2)).reshape(RANK, ACT)
    basis_out = (basis * math.sqrt(ROWS)).reshape(CHANNELS, 2 * PIX, RANK)
    r_factor = lower_factor.T / math.sqrt(ROWS * ACT)
    return (basis_out, projection, r_factor)
```

```python
import functools
import math

import jax
import jax.numpy as jnp
from jax import lax
from jax.experimental import pallas as pl
from jax.experimental.pallas import tpu as pltpu
from jax.sharding import PartitionSpec as P

GRID = 128
FOCAL = 256
RANK = 128
ACT = 32768
PANEL = 8
COLS = 1024

INFL_RATE = 4.5
DEFOCUS_RATE = 6.0
MESH = pl.DeviceIdType.MESH
HIGH = lax.Precision.HIGHEST

SIN_POLY = (4.4428679, -7.30744342, 3.59478808, -0.78437403)
COS_POLY = (1.4142135, -6.97885099, 5.73946117, -1.88356299, 0.310698192)


def split3(value):
    high = lax.reduce_precision(value, 8, 7)
    middle = lax.reduce_precision(value - high, 8, 7)
    low = lax.reduce_precision(value - high - middle, 8, 7)
    return [high, middle, low]


def pixel_features(pixels, wave_scale, flux_level):
    u = (pixels // FOCAL - FOCAL // 2).astype(jnp.float32)
    v = (pixels % FOCAL - FOCAL // 2).astype(jnp.float32)
    radius = u * u + v * v
    amplitude = flux_level * jnp.exp(-INFL_RATE * radius / (FOCAL * FOCAL))
    step_u = -(wave_scale / FOCAL) * u
    step_v = -(wave_scale / FOCAL) * v
    defocus = radius * (DEFOCUS_RATE / (FOCAL * FOCAL)) / wave_scale
    rows = []
    for turns in (step_u, step_v, defocus):
        rows += split3(turns - jnp.round(turns))
    one, zero = jnp.ones_like(u), jnp.zeros_like(u)
    rows += [one] * 3 + [zero] * 4
    high, middle, low = split3(amplitude)
    rows += [high, high, high, middle, middle, low] + [zero] * 10
    return jnp.stack(rows)


def actuator_features(codes, field):
    mirror = (codes // (GRID * GRID)).astype(jnp.float32)
    x = (codes // GRID % GRID - GRID // 2).astype(jnp.float32)
    y = (codes % GRID - GRID // 2).astype(jnp.float32)
    zero = jnp.zeros_like(x)
    angle = jnp.arctan2(field[1], field[0]) * (0.5 / math.pi)
    magnitude = jnp.sqrt(field[0] * field[0] + field[1] * field[1])
    rows = [x] * 3 + [y] * 3 + [mirror] * 3 + split3(angle) + [zero] * 4
    high, middle, low = split3(magnitude)
    rows += [high, middle, low, high, middle, high] + [zero] * 10
    return jnp.stack(rows).astype(jnp.bfloat16)


def dot_first(lhs, rhs, precision=None):
    return lax.dot_general(
        lhs, rhs, (((0,), (0,)), ((), ())), precision=precision, preferred_element_type=jnp.float32
    )


def jacobian_tile(pix, act):
    turns = dot_first(pix[:16], act[:16])
    scale = dot_first(pix[16:], act[16:])
    f = turns - jnp.round(turns)
    q = f * f
    sine = SIN_POLY[-1]
    for coefficient in SIN_POLY[-2::-1]:
        sine = sine * q + coefficient
    sine = sine * f
    cosine = COS_POLY[-1]
    for coefficient in COS_POLY[-2::-1]:
        cosine = cosine * q + coefficient
    real = (scale * (1.0 - sine * sine)).astype(jnp.bfloat16)
    imag = (scale * (sine * cosine)).astype(jnp.bfloat16)
    return jnp.concatenate([real, imag], axis=0)


def kernel(
    A, Z, pix_ref, act_ref, omega_ref, basis_ref, proj_ref, rfac_ref,
    pix_all, act_all, rs_send, rs_recv, own, sk_all, jac, aug, tmat, ex_send, ex_recv,
    feat_s, feat_r, rs_s, rs_r, z_s, z_r, pl_s, pl_r, ex_s, ex_r, local_s,
):
    ai, zi = lax.axis_index("act"), lax.axis_index("pix")
    rows_blk = rs_send.shape[1]
    cols = act_ref.shape[1]
    part = act_all.shape[2]
    share = RANK // Z
    chunk = min(COLS, cols)

    def act_peer(k):
        return lax.rem(ai + k, A)

    def pix_peer(k):
        return lax.rem(zi + k, Z)

    barrier = pltpu.get_barrier_semaphore()

    @pl.loop(1, A)
    def _(k):
        pl.semaphore_signal(barrier, inc=1, device_id=(act_peer(k), zi), device_id_type=MESH)

    for k in range(1, Z):
        pl.semaphore_signal(barrier, inc=1, device_id=(ai, pix_peer(k)), device_id_type=MESH)
    pl.semaphore_wait(barrier, A - 1 + Z - 1)

    def feat_copies(peer, slot):
        return (
            pltpu.make_async_remote_copy(
                src_ref=pix_ref, dst_ref=pix_all.at[slot], send_sem=feat_s.at[peer, 0],
                recv_sem=feat_r.at[slot, 0], device_id=(ai, peer), device_id_type=MESH),
            pltpu.make_async_remote_copy(
                src_ref=act_ref.at[:, pl.ds(pl.multiple_of(peer * part, part), part)],
                dst_ref=act_all.at[slot], send_sem=feat_s.at[peer, 1],
                recv_sem=feat_r.at[slot, 1], device_id=(ai, peer), device_id_type=MESH),
        )

    for k in range(1, Z):
        for copy in feat_copies(pix_peer(k), zi):
            copy.start()
    mine = pl.ds(pl.multiple_of(zi * part, part), part)
    act_all[zi] = act_ref[:, mine]
    pix_all[zi] = pix_ref[...]

    def rs_copy(peer, slot):
        return pltpu.make_async_remote_copy(
            src_ref=rs_send.at[peer], dst_ref=rs_recv.at[slot], send_sem=rs_s.at[peer],
            recv_sem=rs_r.at[slot], device_id=(peer, zi), device_id_type=MESH)

    def partial(block):
        total = jnp.zeros((rows_blk, RANK), jnp.float32)
        for start in range(0, cols, chunk):
            tile = jacobian_tile(pix_ref[block], act_ref[:, start:start + chunk])
            total += jnp.dot(
                tile, omega_ref[start:start + chunk], preferred_element_type=jnp.float32)
        rs_send[block] = total

    @pl.loop(1, A)
    def _(k):
        block = act_peer(k)
        partial(block)
        rs_copy(block, ai).start()

    partial(ai)
    own[...] = rs_send[ai]

    @pl.loop(1, A)
    def _(k):
        peer = act_peer(A - k)
        rs_copy(peer, peer).wait_recv()
        own[...] += rs_recv[peer]

    def block_of(channel, shard):
        return pl.ds(pl.multiple_of((channel * A + shard) * rows_blk, rows_blk), rows_blk)

    def z_copy(peer, slot):
        return pltpu.make_async_remote_copy(
            src_ref=sk_all.at[block_of(slot, ai)], dst_ref=sk_all.at[block_of(slot, ai)],
            send_sem=z_s.at[peer], recv_sem=z_r.at[slot], device_id=(ai, peer), device_id_type=MESH)

    def plane_copy(channel, peer, slot):
        return pltpu.make_async_remote_copy(
            src_ref=sk_all.at[block_of(channel, slot)], dst_ref=sk_all.at[block_of(channel, slot)],
            send_sem=pl_s.at[channel, peer], recv_sem=pl_r.at[channel, slot],
            device_id=(peer, zi), device_id_type=MESH)

    sk_all[block_of(zi, ai)] = own[...].astype(jnp.bfloat16)
    for k in range(1, Z):
        z_copy(pix_peer(k), zi).start()

    def spread(channel):
        @pl.loop(1, A)
        def _(k):
            plane_copy(channel, act_peer(k), ai).start()

    def fill(channel):
        @pl.loop(0, A)
        def _(a):
            jac[block_of(channel, a)] = jacobian_tile(pix_all[channel, a], act_all[channel])

    spread(zi)
    fill(zi)
    for k in range(1, Z):
        z_copy(pix_peer(k), pix_peer(k)).wait_recv()
        spread(pix_peer(k))
    for k in range(1, Z):
        for copy in feat_copies(pix_peer(k), pix_peer(k)):
            copy.wait_recv()
    @pl.loop(1, Z)
    def _(k):
        fill(pix_peer(k))

    @pl.loop(0, Z)
    def _(c):
        @pl.loop(1, A)
        def _(k):
            plane_copy(c, act_peer(k), act_peer(k)).wait_recv()

    sketch = sk_all[...]
    aug[:, :RANK] = dot_first(sketch, sketch)
    row_id = lax.broadcasted_iota(jnp.int32, (RANK, RANK), 0)
    col_id = lax.broadcasted_iota(jnp.int32, (RANK, RANK), 1)
    aug[:, RANK:] = (row_id == col_id).astype(jnp.float32)
    tmat[...] = jnp.zeros_like(tmat)
    panels = RANK // PANEL
    span = sk_all.shape[0] // panels
    sub = lax.broadcasted_iota(jnp.int32, (PANEL, RANK), 0)
    lane = lax.broadcasted_iota(jnp.int32, (PANEL, RANK), 1)

    @pl.loop(0, panels)
    def _(i):
        at = pl.multiple_of(i * PANEL, PANEL)
        left = aug[pl.ds(at, PANEL), :RANK]
        right = aug[pl.ds(at, PANEL), RANK:]
        rolled = pltpu.roll(left, lax.rem(RANK - at, RANK), 1)
        column = [jnp.broadcast_to(rolled[:, k:k + 1], (PANEL, RANK)) for k in range(PANEL)]
        for k in range(PANEL):
            inverse = lax.rsqrt(column[k][k:k + 1])
            weight = jnp.where(sub > k, column[k] * inverse, 0.0)
            left_row, right_row = left[k:k + 1] * inverse, right[k:k + 1] * inverse
            left = jnp.where(sub == k, left_row, left - weight * left_row)
            right = jnp.where(sub == k, right_row, right - weight * right_row)
            for l in range(k + 1, PANEL):
                column[l] = column[l] - weight * (column[l][k:k + 1] * inverse)
        aug[pl.ds(at, PANEL), :RANK] = left
        aug[pl.ds(at, PANEL), RANK:] = right
        factor = jnp.where(lane >= at + PANEL, left, 0.0)
        both = jnp.concatenate([left, right], axis=1)
        aug[...] = aug[...] - dot_first(factor, both, HIGH)
        rows = pl.ds(pl.multiple_of(i * span, span), span)
        tmat[...] += dot_first(sk_all[rows], jac[rows])

    inverse_l = aug[:, RANK:]
    rfac_ref[...] = jnp.where(col_id >= row_id, aug[:, :RANK], 0.0) * (
        1.0 / math.sqrt(rows_blk * A * Z * ACT))
    projection = jnp.dot(inverse_l, tmat[...], precision=HIGH, preferred_element_type=jnp.float32)
    for z in range(Z):
        ex_send[z] = projection[z * share:(z + 1) * share].astype(jnp.bfloat16)

    def ex_copy(peer, slot):
        return pltpu.make_async_remote_copy(
            src_ref=ex_send.at[peer], dst_ref=ex_recv.at[slot], send_sem=ex_s.at[peer],
            recv_sem=ex_r.at[slot], device_id=(ai, peer), device_id_type=MESH)

    for k in range(1, Z):
        ex_copy(pix_peer(k), zi).start()
    basis = lax.dot_general(
        own[...], inverse_l, (((1,), (1,)), ((), ())), precision=HIGH,
        preferred_element_type=jnp.float32)
    basis_ref[...] = basis * math.sqrt(rows_blk * A * Z)
    proj_ref[:, mine] = ex_send[zi].astype(jnp.float32)

    @pl.loop(1, A)
    def _(k):
        rs_copy(act_peer(k), ai).wait_send()

    for k in range(1, Z):
        for copy in feat_copies(pix_peer(k), zi):
            copy.wait_send()
        z_copy(pix_peer(k), zi).wait_send()

    @pl.loop(0, Z)
    def _(c):
        @pl.loop(1, A)
        def _(k):
            plane_copy(c, act_peer(k), ai).wait_send()

    for k in range(1, Z):
        peer = pix_peer(k)
        ex_copy(peer, peer).wait_recv()
        proj_ref[:, pl.ds(pl.multiple_of(peer * part, part), part)] = ex_recv[peer].astype(
            jnp.float32)
    for k in range(1, Z):
        ex_copy(pix_peer(k), zi).wait_send()


def on_device(pixel_index, act_map, omega, pupil_field, channel_scale, channel_flux):
    A, Z = lax.axis_size("act"), lax.axis_size("pix")
    pixels = pixel_index[0]
    count = pixels.shape[0]
    cols = act_map.shape[0]
    part = cols // Z
    block = count // A
    rows_blk = 2 * block
    pix = pixel_features(pixels, channel_scale[0], channel_flux[0])
    pix = pix.reshape(32, A, block).transpose(1, 0, 2).astype(jnp.bfloat16)
    act = actuator_features(act_map, pupil_field[0])
    vmem = pl.BlockSpec(memory_space=pltpu.VMEM)
    dma = pltpu.SemaphoreType.DMA
    f32, bf16 = jnp.float32, jnp.bfloat16
    basis, projection, r_factor = pl.pallas_call(
        functools.partial(kernel, A, Z),
        out_shape=(
            jax.ShapeDtypeStruct((rows_blk, RANK), f32),
            jax.ShapeDtypeStruct((RANK // Z, cols), f32),
            jax.ShapeDtypeStruct((RANK, RANK), f32),
        ),
        in_specs=[vmem] * 3,
        out_specs=(vmem,) * 3,
        scratch_shapes=[
            pltpu.VMEM((Z, A, 32, block), bf16),
            pltpu.VMEM((Z, 32, part), bf16),
            pltpu.VMEM((A, rows_blk, RANK), f32),
            pltpu.VMEM((A, rows_blk, RANK), f32),
            pltpu.VMEM((rows_blk, RANK), f32),
            pltpu.VMEM((Z * A * rows_blk, RANK), bf16),
            pltpu.VMEM((Z * A * rows_blk, part), bf16),
            pltpu.VMEM((RANK, 2 * RANK), f32),
            pltpu.VMEM((RANK, part), f32),
            pltpu.VMEM((Z, RANK // Z, part), bf16),
            pltpu.VMEM((Z, RANK // Z, part), bf16),
            dma((Z, 2)), dma((Z, 2)), dma((A,)), dma((A,)), dma((Z,)), dma((Z,)),
            dma((Z, A)), dma((Z, A)), dma((Z,)), dma((Z,)), dma,
        ],
        compiler_params=pltpu.CompilerParams(
            collective_id=0, has_side_effects=True, vmem_limit_bytes=48 * 1024 * 1024),
    )(pix, act, omega)
    basis_out = basis.reshape(2, block, RANK).transpose(1, 0, 2).reshape(1, rows_blk, RANK)
    return basis_out, projection, r_factor


def solution(mesh):
    return jax.shard_map(
        on_device,
        mesh=mesh,
        in_specs=(
            P("pix", None),
            P("act"),
            P("act", None),
            P("pix", None, "act"),
            P("pix"),
            P("pix"),
        ),
        out_specs=(P("pix", "act", None), P("pix", "act"), P()),
        check_vma=False,
    )
```

```python
import functools
import math

import jax
import jax.numpy as jnp
from jax import lax
from jax.experimental import pallas as pl
from jax.experimental.pallas import tpu as pltpu
from jax.sharding import PartitionSpec as P

GRID = 128
FOCAL = 256
RANK = 128
ACT = 32768
PANEL = 8
COLS = 2048

INFL_RATE = 4.5
DEFOCUS_RATE = 6.0
MESH = pl.DeviceIdType.MESH
HIGH = lax.Precision.HIGHEST

SIN_POLY = (4.4428679, -7.30744342, 3.59478808, -0.78437403)
COS_POLY = (1.4142135, -6.97885099, 5.73946117, -1.88356299, 0.310698192)


def split(value, parts):
    pieces = []
    for _ in range(parts):
        piece = value.astype(jnp.bfloat16).astype(jnp.float32)
        pieces.append(piece)
        value = value - piece
    return pieces


def pixel_features(pixels, wave_scale, flux_level):
    u = (pixels // FOCAL - FOCAL // 2).astype(jnp.float32)
    v = (pixels % FOCAL - FOCAL // 2).astype(jnp.float32)
    radius = u * u + v * v
    amplitude = flux_level * jnp.exp(-INFL_RATE / (FOCAL * FOCAL) * radius)
    step_u = -(wave_scale / FOCAL) * u
    step_v = -(wave_scale / FOCAL) * v
    defocus = radius * (DEFOCUS_RATE / (FOCAL * FOCAL)) / wave_scale
    rows = []
    for turns, parts in ((step_u, 3), (step_v, 3), (defocus, 2)):
        rows += split(turns - jnp.round(turns), parts)
    one, zero = jnp.ones_like(u), jnp.zeros_like(u)
    high, low = split(amplitude, 2)
    return rows + [one, one, high, high, low, low, zero, zero]


def actuator_features(codes, field_re, field_im):
    mirror = (codes // (GRID * GRID)).astype(jnp.float32)
    x = (codes // GRID % GRID - GRID // 2).astype(jnp.float32)
    y = (codes % GRID - GRID // 2).astype(jnp.float32)
    zero = jnp.zeros_like(x)
    angle = jnp.arctan2(field_im, field_re) * (0.5 / math.pi)
    high, low = split(jnp.sqrt(field_re * field_re + field_im * field_im), 2)
    return [x] * 3 + [y] * 3 + [mirror] * 2 + split(angle, 2) + [high, low, high, low, zero, zero]


def dot_first(lhs, rhs, precision=None):
    return lax.dot_general(
        lhs, rhs, (((0,), (0,)), ((), ())), precision=precision, preferred_element_type=jnp.float32
    )


def jacobian_tile(pix, act):
    row = lax.broadcasted_iota(jnp.int32, pix.shape, 0)
    none = jnp.zeros_like(pix)
    turns = dot_first(jnp.where(row < 10, pix, none), act)
    scale = dot_first(jnp.where(row < 10, none, pix), act)
    f = turns - jnp.round(turns)
    q = f * f
    sine = SIN_POLY[-1]
    for coefficient in SIN_POLY[-2::-1]:
        sine = sine * q + coefficient
    sine = sine * f
    cosine = COS_POLY[-1]
    for coefficient in COS_POLY[-2::-1]:
        cosine = cosine * q + coefficient
    real = (scale * (1.0 - sine * sine)).astype(jnp.bfloat16)
    imag = (scale * (sine * cosine)).astype(jnp.bfloat16)
    return jnp.concatenate([real, imag], axis=0)


def kernel(
    A, Z, index_ref, codes_ref, field_ref, scale_ref, flux_ref, omega_ref, basis_ref, proj_ref, rfac_ref,
    rows_ref, pix_ref, act_ref, pix_all, act_all, rs_send, rs_recv, own, sk_all, jac, aug, tmat, ex_send, ex_recv,
    feat_s, feat_r, rs_s, rs_r, z_s, z_r, pl_s, pl_r, sib_s, ex_s, ex_r,
):
    ai, zi = lax.axis_index("act"), lax.axis_index("pix")
    rows_blk = rs_send.shape[1]
    cols = act_ref.shape[1]
    part = act_all.shape[2]
    share = RANK // Z
    chunk = min(COLS, cols)

    def act_peer(k):
        return lax.rem(ai + k, A)

    def pix_peer(k):
        return lax.rem(zi + k, Z)

    barrier = pltpu.get_barrier_semaphore()

    @pl.loop(1, A)
    def _(k):
        pl.semaphore_signal(barrier, inc=1, device_id=(act_peer(k), zi), device_id_type=MESH)

    for k in range(1, Z):
        pl.semaphore_signal(barrier, inc=1, device_id=(ai, pix_peer(k)), device_id_type=MESH)

    block = pix_ref.shape[2]
    for at, row in enumerate(pixel_features(index_ref[...], scale_ref[0], flux_ref[0])):
        rows_ref[at:at + 1, :A * block] = row
    for a in range(A):
        pix_ref[a] = rows_ref[:, a * block:(a + 1) * block].astype(jnp.bfloat16)
    features = actuator_features(codes_ref[...], field_ref[0, 0:1], field_ref[0, 1:2])
    for at, row in enumerate(features):
        rows_ref[at:at + 1, :cols] = row
    act_ref[...] = rows_ref[:, :cols].astype(jnp.bfloat16)
    pl.semaphore_wait(barrier, A - 1 + Z - 1)

    def feat_copies(peer, slot):
        return (
            pltpu.make_async_remote_copy(
                src_ref=pix_ref, dst_ref=pix_all.at[slot], send_sem=feat_s.at[peer, 0],
                recv_sem=feat_r.at[slot, 0], device_id=(ai, peer), device_id_type=MESH),
            pltpu.make_async_remote_copy(
                src_ref=act_ref.at[:, pl.ds(pl.multiple_of(peer * part, part), part)],
                dst_ref=act_all.at[slot], send_sem=feat_s.at[peer, 1],
                recv_sem=feat_r.at[slot, 1], device_id=(ai, peer), device_id_type=MESH),
        )

    for k in range(1, Z):
        for copy in feat_copies(pix_peer(k), zi):
            copy.start()
    mine = pl.ds(pl.multiple_of(zi * part, part), part)
    act_all[zi] = act_ref[:, mine]
    pix_all[zi] = pix_ref[...]

    def rs_copy(peer, slot):
        return pltpu.make_async_remote_copy(
            src_ref=rs_send.at[peer], dst_ref=rs_recv.at[slot], send_sem=rs_s.at[peer],
            recv_sem=rs_r.at[slot], device_id=(peer, zi), device_id_type=MESH)

    def partial(block):
        total = jnp.zeros((rows_blk, RANK), jnp.float32)
        for start in range(0, cols, chunk):
            tile = jacobian_tile(pix_ref[block], act_ref[:, start:start + chunk])
            total += jnp.dot(
                tile, omega_ref[start:start + chunk], preferred_element_type=jnp.float32)
        rs_send[block] = total

    @pl.loop(1, A)
    def _(k):
        block = act_peer(k)
        partial(block)
        rs_copy(block, ai).start()

    partial(ai)
    own[...] = rs_send[ai]

    @pl.loop(1, A)
    def _(k):
        peer = act_peer(A - k)
        rs_copy(peer, peer).wait_recv()
        own[...] += rs_recv[peer]

    def block_of(channel, shard):
        return pl.ds(pl.multiple_of((channel * A + shard) * rows_blk, rows_blk), rows_blk)

    def z_copy(peer, slot):
        return pltpu.make_async_remote_copy(
            src_ref=sk_all.at[block_of(slot, ai)], dst_ref=sk_all.at[block_of(slot, ai)],
            send_sem=z_s.at[peer], recv_sem=z_r.at[slot], device_id=(ai, peer), device_id_type=MESH)

    def plane_copy(channel, peer, slot):
        return pltpu.make_async_remote_copy(
            src_ref=sk_all.at[block_of(channel, slot)], dst_ref=sk_all.at[block_of(channel, slot)],
            send_sem=pl_s.at[channel, peer], recv_sem=pl_r.at[channel, slot],
            device_id=(peer, zi), device_id_type=MESH)

    sk_all[block_of(zi, ai)] = own[...].astype(jnp.bfloat16)
    for k in range(1, Z):
        z_copy(pix_peer(k), zi).start()

    sibling = ai + 1 - 2 * lax.rem(ai, 2)

    def spread(channel):
        @pl.loop(1, A // 2)
        def _(k):
            plane_copy(channel, act_peer(2 * k), ai).start()

        pass_on(channel, ai).start()

    def pass_on(channel, shard):
        return pltpu.make_async_remote_copy(
            src_ref=sk_all.at[block_of(channel, shard)], dst_ref=sk_all.at[block_of(channel, shard)],
            send_sem=sib_s.at[channel, shard], recv_sem=pl_r.at[channel, shard],
            device_id=(sibling, zi), device_id_type=MESH)

    def forward(channel):
        @pl.loop(1, A // 2)
        def _(k):
            shard = act_peer(2 * k)
            plane_copy(channel, shard, shard).wait_recv()
            pass_on(channel, shard).start()

    def fill(channel):
        @pl.loop(0, A)
        def _(a):
            jac[block_of(channel, a)] = jacobian_tile(pix_all[channel, a], act_all[channel])

    early = Z // 2
    spread(zi)
    fill(zi)
    for k in range(1, Z):
        z_copy(pix_peer(k), pix_peer(k)).wait_recv()
        spread(pix_peer(k))
    forward(zi)
    for k in range(1, Z):
        for copy in feat_copies(pix_peer(k), pix_peer(k)):
            copy.wait_recv()
    for k in range(1, early):
        fill(pix_peer(k))

    @pl.loop(1, Z)
    def _(k):
        forward(pix_peer(k))

    @pl.loop(0, Z)
    def _(c):
        @pl.loop(0, A // 2)
        def _(k):
            shard = lax.rem(sibling + 2 * k, A)
            pass_on(c, shard).wait_recv()

    sketch = sk_all[...]
    aug[:, :RANK] = dot_first(sketch, sketch)
    row_id = lax.broadcasted_iota(jnp.int32, (RANK, RANK), 0)
    col_id = lax.broadcasted_iota(jnp.int32, (RANK, RANK), 1)
    aug[:, RANK:] = (row_id == col_id).astype(jnp.float32)
    tmat[...] = jnp.zeros_like(tmat)
    panels = RANK // PANEL
    late = (Z - early) * A // panels
    sub = lax.broadcasted_iota(jnp.int32, (PANEL, RANK), 0)
    lane = lax.broadcasted_iota(jnp.int32, (PANEL, RANK), 1)

    @pl.loop(0, panels)
    def _(i):
        at = pl.multiple_of(i * PANEL, PANEL)
        left = aug[pl.ds(at, PANEL), :RANK]
        right = aug[pl.ds(at, PANEL), RANK:]
        rolled = pltpu.roll(left, lax.rem(RANK - at, RANK), 1)
        column = [jnp.broadcast_to(rolled[:, k:k + 1], (PANEL, RANK)) for k in range(PANEL)]
        for k in range(PANEL):
            inverse = lax.rsqrt(column[k][k:k + 1])
            weight = jnp.where(sub > k, column[k] * inverse, 0.0)
            left_row, right_row = left[k:k + 1] * inverse, right[k:k + 1] * inverse
            left = jnp.where(sub == k, left_row, left - weight * left_row)
            right = jnp.where(sub == k, right_row, right - weight * right_row)
            for l in range(k + 1, PANEL):
                column[l] = column[l] - weight * (column[l][k:k + 1] * inverse)
        aug[pl.ds(at, PANEL), :RANK] = left
        aug[pl.ds(at, PANEL), RANK:] = right
        factor = jnp.where(lane >= at + PANEL, left, 0.0)
        both = jnp.concatenate([left, right], axis=1)
        aug[...] = aug[...] - dot_first(factor, both, HIGH)
        for n in range(late):
            at = i * late + n
            done = block_of(pix_peer(at // A), lax.rem(at, A))
            tmat[...] += dot_first(sk_all[done], jac[done])
            channel, shard = pix_peer(early + at // A), lax.rem(at, A)
            tile = jacobian_tile(pix_all[channel, shard], act_all[channel])
            tmat[...] += dot_first(sk_all[block_of(channel, shard)], tile)

    inverse_l = aug[:, RANK:]
    rfac_ref[...] = jnp.where(col_id >= row_id, aug[:, :RANK], 0.0) * (
        1.0 / math.sqrt(rows_blk * A * Z * ACT))
    projection = jnp.dot(inverse_l, tmat[...], precision=HIGH, preferred_element_type=jnp.float32)
    for z in range(Z):
        ex_send[z] = projection[z * share:(z + 1) * share].astype(jnp.bfloat16)

    def ex_copy(peer, slot):
        return pltpu.make_async_remote_copy(
            src_ref=ex_send.at[peer], dst_ref=ex_recv.at[slot], send_sem=ex_s.at[peer],
            recv_sem=ex_r.at[slot], device_id=(ai, peer), device_id_type=MESH)

    for k in range(1, Z):
        ex_copy(pix_peer(k), zi).start()
    basis = lax.dot_general(
        own[...], inverse_l, (((1,), (1,)), ((), ())), precision=HIGH,
        preferred_element_type=jnp.float32)
    basis_ref[...] = basis * math.sqrt(rows_blk * A * Z)
    proj_ref[:, mine] = ex_send[zi].astype(jnp.float32)

    @pl.loop(1, A)
    def _(k):
        rs_copy(act_peer(k), ai).wait_send()

    for k in range(1, Z):
        for copy in feat_copies(pix_peer(k), zi):
            copy.wait_send()
        z_copy(pix_peer(k), zi).wait_send()

    @pl.loop(0, Z)
    def _(c):
        @pl.loop(1, A // 2)
        def _(k):
            plane_copy(c, act_peer(2 * k), ai).wait_send()

        @pl.loop(0, A // 2)
        def _(k):
            pass_on(c, act_peer(2 * k)).wait_send()

    for k in range(1, Z):
        peer = pix_peer(k)
        ex_copy(peer, peer).wait_recv()
        proj_ref[:, pl.ds(pl.multiple_of(peer * part, part), part)] = ex_recv[peer].astype(
            jnp.float32)
    for k in range(1, Z):
        ex_copy(pix_peer(k), zi).wait_send()


def on_device(pixel_index, act_map, omega, pupil_field, channel_scale, channel_flux):
    A, Z = lax.axis_size("act"), lax.axis_size("pix")
    count = pixel_index.shape[1]
    cols = act_map.shape[0]
    part = cols // Z
    block = count // A
    rows_blk = 2 * block
    vmem = pl.BlockSpec(memory_space=pltpu.VMEM)
    smem = pl.BlockSpec(memory_space=pltpu.SMEM)
    dma = pltpu.SemaphoreType.DMA
    f32, bf16 = jnp.float32, jnp.bfloat16
    basis, projection, r_factor = pl.pallas_call(
        functools.partial(kernel, A, Z),
        out_shape=(
            jax.ShapeDtypeStruct((rows_blk, RANK), f32),
            jax.ShapeDtypeStruct((RANK // Z, cols), f32),
            jax.ShapeDtypeStruct((RANK, RANK), f32),
        ),
        in_specs=[vmem] * 3 + [smem] * 2 + [vmem],
        out_specs=(vmem,) * 3,
        scratch_shapes=[
            pltpu.VMEM((16, max(cols, count)), f32),
            pltpu.VMEM((A, 16, block), bf16),
            pltpu.VMEM((16, cols), bf16),
            pltpu.VMEM((Z, A, 16, block), bf16),
            pltpu.VMEM((Z, 16, part), bf16),
            pltpu.VMEM((A, rows_blk, RANK), f32),
            pltpu.VMEM((A, rows_blk, RANK), f32),
            pltpu.VMEM((rows_blk, RANK), f32),
            pltpu.VMEM((Z * A * rows_blk, RANK), bf16),
            pltpu.VMEM((Z * A * rows_blk, part), bf16),
            pltpu.VMEM((RANK, 2 * RANK), f32),
            pltpu.VMEM((RANK, part), f32),
            pltpu.VMEM((Z, RANK // Z, part), bf16),
            pltpu.VMEM((Z, RANK // Z, part), bf16),
            dma((Z, 2)), dma((Z, 2)), dma((A,)), dma((A,)), dma((Z,)), dma((Z,)),
            dma((Z, A)), dma((Z, A)), dma((Z, A)), dma((Z,)), dma((Z,)),
        ],
        compiler_params=pltpu.CompilerParams(
            collective_id=0, has_side_effects=True, vmem_limit_bytes=48 * 1024 * 1024),
    )(pixel_index, act_map.reshape(1, cols), pupil_field, channel_scale, channel_flux, omega)
    basis_out = basis.reshape(2, block, RANK).transpose(1, 0, 2).reshape(1, rows_blk, RANK)
    return basis_out, projection, r_factor


def solution(mesh):
    return jax.shard_map(
        on_device,
        mesh=mesh,
        in_specs=(
            P("pix", None),
            P("act"),
            P("act", None),
            P("pix", None, "act"),
            P("pix"),
            P("pix"),
        ),
        out_specs=(P("pix", "act", None), P("pix", "act"), P()),
        check_vma=False,
    )
```
